32 devices in a mesh: seq: 8 (over y, x, core), mp: 4 (over z).
Axes of the slice: x: 2, y: 2, z: 4, core: 2. Of those that a mesh axis runs over, the one named last changes fastest.
Arguments:
- tokens: bfloat16 [1024, 4096], P('seq', 'mp'), may hold values from -6 to 6
- w_proj: bfloat16 [4096, 3, 2048], P('seq', None, 'mp'), may hold values from -0.09375 to 0.09375
- short_filter: float32 [3, 3, 2048], P(None, None, 'mp'), may hold values from -3.5 to 3.5
- long_filter: float32 [2048, 1024], P(('mp', 'seq')), may hold values from -0.1875 to 0.1875
- skip_gain: float32 [2048], P('mp'), may hold values from -4 to 4
Outputs:
- gated: bfloat16 [1024, 2048], P('seq', 'mp')
The draws below stay inside these ranges and needn't reach their ends.
All inputs are finite; a program needn't handle non-finite values.
Results may differ from the reference program's by a relative error of at most 0.012.
Values may be sent and summed in bfloat16 or wider, within the bound.
A program may use at most 64 MiB of HBM per device.

```python
import math
import jax
import jax.numpy as jnp
from jax import lax

D = 4096
CH = 2048
KS = 3
SEQLEN = 1024


def levels(own_key, dims, shards, least, high):
    level, own = 1.0, jax.random.fold_in(own_key, 6)
    for position, blocks in shards:
        steps = jnp.exp(jax.random.uniform(jax.random.fold_in(own, position), (blocks,), jnp.float32, least / len(shards), high / len(shards)))
        level = level * jnp.repeat(steps, dims[position] // blocks).reshape([-1 if axis == position else 1 for axis in range(len(dims))])
    return level


def noise(key, extent, deviation, bound, shards=(), kind=jnp.bfloat16):
    loudness = levels(key, extent, shards, -0.22, 0.18) if shards else 1.0
    entries = jax.random.normal(key, extent, jnp.float32) * deviation * loudness
    return jnp.minimum(jnp.maximum(entries, -bound), bound).astype(kind)


def setup_inputs(seed: int = 0) -> dict:
    keys = jax.random.split(jax.random.key(seed), 6)
    tokens = noise(keys[0], (SEQLEN, D), 1.0, 6.0, ((0, 8), (1, 4)))
    w_proj = noise(keys[1], (D, 3, CH), D ** -0.5, 0.09375, ((0, 8), (2, 4)))
    short_filter = noise(keys[2], (3, KS, CH), KS ** -0.5, 3.5, ((2, 4),), jnp.float32)
    long_filter = noise(keys[3], (CH, SEQLEN), SEQLEN ** -0.5, 0.1875, ((0, 32),), jnp.float32)
    skip_gain = noise(keys[4], (CH,), 1.0, 4.0, ((0, 4),), jnp.float32)
    return dict(tokens=tokens, w_proj=w_proj, short_filter=short_filter, long_filter=long_filter, skip_gain=skip_gain)


def reference(tokens, w_proj, short_filter, long_filter, skip_gain):
    branches = []
    for member in range(3):
        projected = jnp.dot(tokens, w_proj[:, member, :], preferred_element_type=jnp.float32).astype(jnp.bfloat16)
        padded = jnp.pad(projected.astype(jnp.float32), ((KS - 1, 0), (0, 0)))
        mixed = jnp.zeros((SEQLEN, CH), jnp.float32)
        for offset in range(KS):
            mixed = mixed + short_filter[member, offset][None, :] * padded[KS - 1 - offset:KS - 1 - offset + SEQLEN]
        branches.append(mixed)
    query_rows, key_rows, value_rows = branches
    product = (key_rows * value_rows).astype(jnp.bfloat16)
    blocked = math.gcd(CH, 128)
    channel_major = product.astype(jnp.float32).T.reshape(CH // blocked, blocked, SEQLEN)
    filter_major = long_filter.reshape(CH // blocked, blocked, SEQLEN)
    padded_len = 2 * SEQLEN

    def convolve(pair):
        signal, kernel = pair
        spectrum = jnp.fft.rfft(signal, n=padded_len) * jnp.fft.rfft(kernel, n=padded_len)
        return jnp.fft.irfft(spectrum, n=padded_len)[:, :SEQLEN]

    convolved = lax.map(convolve, (channel_major, filter_major)).reshape(CH, SEQLEN).T.astype(jnp.bfloat16)
    result = query_rows * (convolved.astype(jnp.float32) + skip_gain[None, :] * product.astype(jnp.float32))
    return result.astype(jnp.bfloat16)
```

```python
import math

import jax
import jax.numpy as jnp
import numpy as np
from jax import lax
from jax.sharding import PartitionSpec as P


def shifted(value, axis, steps):
    count = lax.axis_size(axis)
    leading, last = (max(0, -steps), min(count, count - steps))
    return lax.ppermute(value, axis, [(source, source + steps) for source in range(leading, last)])


def transform(real_part, imag_part, orient, filled):
    length = real_part.shape[-1]
    first = math.gcd(length, 64)
    highest = lax.Precision.HIGHEST
    if length <= 64 or first == 1:
        counter = jnp.arange(length, dtype=jnp.int32)
        angles = (
            2.0
            * math.pi
            / length
            * (counter[:, None] * counter[None, :] % length).astype(jnp.float32)
        )
        cosine = jnp.cos(angles)
        sine = jnp.sin(angles)
        new_real = jnp.dot(real_part, cosine, precision=highest) - orient * jnp.dot(
            imag_part, sine, precision=highest
        )
        new_imag = jnp.dot(imag_part, cosine, precision=highest) + orient * jnp.dot(
            real_part, sine, precision=highest
        )
        return (new_real, new_imag)
    second = length // first
    outer = real_part.shape[:-1]
    live = first
    if filled > 0 and filled % second == 0:
        live = filled // second
    real_grid = real_part.reshape(outer + (first, second))[..., :live, :]
    imag_grid = imag_part.reshape(outer + (first, second))[..., :live, :]
    counter = jnp.arange(first, dtype=jnp.int32)
    angles = (
        2.0 * math.pi / first * (counter[:, None] * counter[None, :] % first).astype(jnp.float32)
    )
    cosine = jnp.cos(angles)[:live]
    sine = jnp.sin(angles)[:live]
    section_real = jnp.einsum(
        "...ab,ak->...kb", real_grid, cosine, precision=highest
    ) - orient * jnp.einsum("...ab,ak->...kb", imag_grid, sine, precision=highest)
    section_imag = jnp.einsum(
        "...ab,ak->...kb", imag_grid, cosine, precision=highest
    ) + orient * jnp.einsum("...ab,ak->...kb", real_grid, sine, precision=highest)
    freq_rows = jnp.arange(first, dtype=jnp.int32)[:, None]
    time_cols = jnp.arange(second, dtype=jnp.int32)[None, :]
    twiddle = 2.0 * math.pi / length * (freq_rows * time_cols).astype(jnp.float32)
    twist_cos = jnp.cos(twiddle)
    twist_sin = jnp.sin(twiddle)
    turned_real = section_real * twist_cos - orient * section_imag * twist_sin
    turned_imag = section_imag * twist_cos + orient * section_real * twist_sin
    inner_real, inner_imag = transform(turned_real, turned_imag, orient, 0)
    final_real = jnp.swapaxes(inner_real, -1, -2).reshape(outer + (length,))
    final_imag = jnp.swapaxes(inner_imag, -1, -2).reshape(outer + (length,))
    return (final_real, final_imag)


def mirrored(values):
    return jnp.concatenate([values[:, :1], values[:, :0:-1]], axis=1)


def long_conv(signal, kernel):
    seq_len = signal.shape[-1]
    padded_signal = jnp.pad(signal.astype(jnp.float32), ((0, 0), (0, seq_len)))
    padded_kernel = jnp.pad(kernel, ((0, 0), (0, seq_len)))
    joint_real, joint_imag = transform(padded_signal, padded_kernel, -1.0, seq_len)
    mirror_real = mirrored(joint_real)
    mirror_imag = mirrored(joint_imag)
    signal_real = 0.5 * (joint_real + mirror_real)
    signal_imag = 0.5 * (joint_imag - mirror_imag)
    kernel_real = 0.5 * (joint_imag + mirror_imag)
    kernel_imag = -0.5 * (joint_real - mirror_real)
    prod_real = signal_real * kernel_real - signal_imag * kernel_imag
    prod_imag = signal_real * kernel_imag + signal_imag * kernel_real
    back_real, back_imag = transform(prod_real, prod_imag, 1.0, 0)
    return back_real[:, :seq_len] / (2.0 * seq_len)


def by_weights(tokens, w_proj, short_filter, long_filter, skip_gain):
    rows_dev = tokens.shape[0]
    margin = short_filter.shape[1] - 1
    width = w_proj.shape[2]
    source = lax.all_gather(tokens, "mp", axis=1, tiled=True)
    projected = jnp.einsum(
        "td,dpc->tpc",
        source,
        lax.all_gather(w_proj, "seq", axis=0, tiled=True),
        preferred_element_type=jnp.float32,
    ).astype(jnp.bfloat16)
    tail = shifted(projected[rows_dev - margin :], "seq", 1)
    extended = jnp.concatenate([tail, projected], axis=0).astype(jnp.float32)
    mixed = jnp.zeros((rows_dev, 3, width), jnp.float32)
    for offset in range(margin + 1):
        mixed = (
            mixed
            + short_filter[:, offset, :][None]
            * extended[margin - offset : margin - offset + rows_dev]
        )
    query_rows = mixed[:, 0]
    product = (mixed[:, 1] * mixed[:, 2]).astype(jnp.bfloat16)
    groups = lax.axis_size("seq")
    channel_count = width // groups
    outgoing = product.reshape(rows_dev, groups, channel_count).transpose(1, 2, 0)
    arrived = lax.all_to_all(outgoing, "seq", split_axis=0, concat_axis=2, tiled=True)[0]
    convolved = long_conv(arrived, long_filter).astype(jnp.bfloat16)[None]
    returned = lax.all_to_all(convolved, "seq", split_axis=2, concat_axis=0, tiled=True)
    back_rows = returned.transpose(2, 0, 1).reshape(rows_dev, width)
    result = query_rows * (
        back_rows.astype(jnp.float32) + skip_gain[None, :] * product.astype(jnp.float32)
    )
    return result.astype(jnp.bfloat16)


def split_float(value):
    high = value.astype(jnp.bfloat16)
    low = (value - high.astype(jnp.float32)).astype(jnp.bfloat16)
    return high, low


def dft_tables(length):
    phase = (4 * np.arange(length)[:, None] + 1) * np.arange(length)[None, :] % (4 * length)
    angles = phase * (2.0 * np.pi / (4 * length))
    table = np.concatenate([np.cos(angles), np.sin(angles)], axis=0).astype(np.float32)
    high = table.astype(jnp.bfloat16)
    low = (table - high.astype(np.float32)).astype(jnp.bfloat16)
    return high, low


def matmul_t(left, right):
    return lax.dot_general(
        left, right, (((1,), (1,)), ((), ())), preferred_element_type=jnp.float32
    )


def matmul(left, right):
    return jnp.dot(left, right, preferred_element_type=jnp.float32)


def filter_spectrum(kernel, tables):
    high, low = tables
    count = kernel.shape[0]
    kernel_high, kernel_low = split_float(kernel)
    both = matmul_t(jnp.concatenate([kernel_high, kernel_low], axis=0), high)
    return both[:count] + both[count:] + matmul_t(kernel_high, low)


def dense_conv(signal, spectrum, tables):
    high, low = tables
    count, length = signal.shape
    own = matmul_t(signal, high) + matmul_t(signal, low)
    own_real, own_imag = own[:, :length], own[:, length:]
    real, imag = spectrum[:, :length], spectrum[:, length:]
    prod = jnp.concatenate(
        [own_real * real - own_imag * imag, own_real * imag + own_imag * real], axis=1
    )
    prod_high, prod_low = split_float(prod)
    both = matmul(jnp.concatenate([prod_high, prod_low], axis=0), high)
    return (both[:count] + both[count:] + matmul(prod_high, low)) * (1.0 / length)


def by_tokens(tokens, w_proj, short_filter, long_filter, skip_gain):
    depth, branches, width = w_proj.shape
    groups = lax.axis_size("seq")
    own = width // groups
    length = tokens.shape[0] * groups
    tables = tuple(jnp.asarray(part) for part in dft_tables(length))
    first = lax.axis_index("seq") * own
    taps = lax.dynamic_slice_in_dim(short_filter, first, own, axis=2)
    gain = lax.dynamic_slice_in_dim(skip_gain, first, own, axis=0)
    spectrum = filter_spectrum(long_filter, tables)
    source = lax.all_gather(tokens, "mp", axis=1, tiled=True)
    features = lax.all_to_all(source, "seq", split_axis=1, concat_axis=0, tiled=True)
    partial = lax.dot_general(
        w_proj.reshape(depth, branches * width),
        features,
        (((0,), (1,)), ((), ())),
        preferred_element_type=jnp.float32,
    ).astype(jnp.bfloat16)
    partial = partial.reshape(branches, groups, own, length)
    terms = lax.all_to_all(partial, "seq", split_axis=1, concat_axis=1, tiled=True)
    projected = jnp.sum(terms.astype(jnp.float32), axis=1).astype(jnp.bfloat16)
    margin = short_filter.shape[1] - 1
    padded = jnp.pad(projected.astype(jnp.float32), ((0, 0), (0, 0), (margin, 0)))
    mixed = jnp.zeros((branches, own, length), jnp.float32)
    for offset in range(margin + 1):
        mixed = mixed + taps[:, offset, :, None] * padded[:, :, margin - offset : margin - offset + length]
    product = (mixed[1] * mixed[2]).astype(jnp.bfloat16)
    convolved = dense_conv(product, spectrum, tables).astype(jnp.bfloat16).astype(jnp.float32)
    result = mixed[0] * (convolved + gain[:, None] * product.astype(jnp.float32))
    returned = lax.all_to_all(
        result.astype(jnp.bfloat16), "seq", split_axis=1, concat_axis=0, tiled=True
    )
    return returned.T


def on_device(tokens, w_proj, short_filter, long_filter, skip_gain):
    if tokens.shape[0] < w_proj.shape[0]:
        return by_tokens(tokens, w_proj, short_filter, long_filter, skip_gain)
    return by_weights(tokens, w_proj, short_filter, long_filter, skip_gain)


def solution(mesh):
    return jax.shard_map(
        on_device,
        mesh=mesh,
        in_specs=(
            P("seq", "mp"),
            P("seq", None, "mp"),
            P(None, None, "mp"),
            P(("mp", "seq"), None),
            P("mp"),
        ),
        out_specs=P("seq", "mp"),
        check_vma=False,
    )
```

```python
import math

import jax
import jax.numpy as jnp
import numpy as np
from jax import lax
from jax.experimental import pallas as pl
from jax.experimental.pallas import tpu as pltpu
from jax.sharding import PartitionSpec as P


def shifted(value, axis, steps):
    count = lax.axis_size(axis)
    leading, last = (max(0, -steps), min(count, count - steps))
    return lax.ppermute(value, axis, [(source, source + steps) for source in range(leading, last)])


def transform(real_part, imag_part, orient, filled):
    length = real_part.shape[-1]
    first = math.gcd(length, 64)
    highest = lax.Precision.HIGHEST
    if length <= 64 or first == 1:
        counter = jnp.arange(length, dtype=jnp.int32)
        angles = (
            2.0
            * math.pi
            / length
            * (counter[:, None] * counter[None, :] % length).astype(jnp.float32)
        )
        cosine = jnp.cos(angles)
        sine = jnp.sin(angles)
        new_real = jnp.dot(real_part, cosine, precision=highest) - orient * jnp.dot(
            imag_part, sine, precision=highest
        )
        new_imag = jnp.dot(imag_part, cosine, precision=highest) + orient * jnp.dot(
            real_part, sine, precision=highest
        )
        return (new_real, new_imag)
    second = length // first
    outer = real_part.shape[:-1]
    live = first
    if filled > 0 and filled % second == 0:
        live = filled // second
    real_grid = real_part.reshape(outer + (first, second))[..., :live, :]
    imag_grid = imag_part.reshape(outer + (first, second))[..., :live, :]
    counter = jnp.arange(first, dtype=jnp.int32)
    angles = (
        2.0 * math.pi / first * (counter[:, None] * counter[None, :] % first).astype(jnp.float32)
    )
    cosine = jnp.cos(angles)[:live]
    sine = jnp.sin(angles)[:live]
    section_real = jnp.einsum(
        "...ab,ak->...kb", real_grid, cosine, precision=highest
    ) - orient * jnp.einsum("...ab,ak->...kb", imag_grid, sine, precision=highest)
    section_imag = jnp.einsum(
        "...ab,ak->...kb", imag_grid, cosine, precision=highest
    ) + orient * jnp.einsum("...ab,ak->...kb", real_grid, sine, precision=highest)
    freq_rows = jnp.arange(first, dtype=jnp.int32)[:, None]
    time_cols = jnp.arange(second, dtype=jnp.int32)[None, :]
    twiddle = 2.0 * math.pi / length * (freq_rows * time_cols).astype(jnp.float32)
    twist_cos = jnp.cos(twiddle)
    twist_sin = jnp.sin(twiddle)
    turned_real = section_real * twist_cos - orient * section_imag * twist_sin
    turned_imag = section_imag * twist_cos + orient * section_real * twist_sin
    inner_real, inner_imag = transform(turned_real, turned_imag, orient, 0)
    final_real = jnp.swapaxes(inner_real, -1, -2).reshape(outer + (length,))
    final_imag = jnp.swapaxes(inner_imag, -1, -2).reshape(outer + (length,))
    return (final_real, final_imag)


def mirrored(values):
    return jnp.concatenate([values[:, :1], values[:, :0:-1]], axis=1)


def long_conv(signal, kernel):
    seq_len = signal.shape[-1]
    padded_signal = jnp.pad(signal.astype(jnp.float32), ((0, 0), (0, seq_len)))
    padded_kernel = jnp.pad(kernel, ((0, 0), (0, seq_len)))
    joint_real, joint_imag = transform(padded_signal, padded_kernel, -1.0, seq_len)
    mirror_real = mirrored(joint_real)
    mirror_imag = mirrored(joint_imag)
    signal_real = 0.5 * (joint_real + mirror_real)
    signal_imag = 0.5 * (joint_imag - mirror_imag)
    kernel_real = 0.5 * (joint_imag + mirror_imag)
    kernel_imag = -0.5 * (joint_real - mirror_real)
    prod_real = signal_real * kernel_real - signal_imag * kernel_imag
    prod_imag = signal_real * kernel_imag + signal_imag * kernel_real
    back_real, back_imag = transform(prod_real, prod_imag, 1.0, 0)
    return back_real[:, :seq_len] / (2.0 * seq_len)


def by_weights(tokens, w_proj, short_filter, long_filter, skip_gain):
    rows_dev = tokens.shape[0]
    margin = short_filter.shape[1] - 1
    width = w_proj.shape[2]
    source = lax.all_gather(tokens, "mp", axis=1, tiled=True)
    projected = jnp.einsum(
        "td,dpc->tpc",
        source,
        lax.all_gather(w_proj, "seq", axis=0, tiled=True),
        preferred_element_type=jnp.float32,
    ).astype(jnp.bfloat16)
    tail = shifted(projected[rows_dev - margin :], "seq", 1)
    extended = jnp.concatenate([tail, projected], axis=0).astype(jnp.float32)
    mixed = jnp.zeros((rows_dev, 3, width), jnp.float32)
    for offset in range(margin + 1):
        mixed = (
            mixed
            + short_filter[:, offset, :][None]
            * extended[margin - offset : margin - offset + rows_dev]
        )
    query_rows = mixed[:, 0]
    product = (mixed[:, 1] * mixed[:, 2]).astype(jnp.bfloat16)
    groups = lax.axis_size("seq")
    channel_count = width // groups
    outgoing = product.reshape(rows_dev, groups, channel_count).transpose(1, 2, 0)
    arrived = lax.all_to_all(outgoing, "seq", split_axis=0, concat_axis=2, tiled=True)[0]
    convolved = long_conv(arrived, long_filter).astype(jnp.bfloat16)[None]
    returned = lax.all_to_all(convolved, "seq", split_axis=2, concat_axis=0, tiled=True)
    back_rows = returned.transpose(2, 0, 1).reshape(rows_dev, width)
    result = query_rows * (
        back_rows.astype(jnp.float32) + skip_gain[None, :] * product.astype(jnp.float32)
    )
    return result.astype(jnp.bfloat16)


def split_float(value):
    high = value.astype(jnp.bfloat16)
    low = (value - high.astype(jnp.float32)).astype(jnp.bfloat16)
    return high, low


def dft_tables(length):
    phase = (4 * np.arange(length)[:, None] + 1) * np.arange(length)[None, :] % (4 * length)
    angles = phase * (2.0 * np.pi / (4 * length))
    table = np.concatenate([np.cos(angles), np.sin(angles)], axis=0).astype(np.float32)
    high = table.astype(jnp.bfloat16)
    low = (table - high.astype(np.float32)).astype(jnp.bfloat16)
    return high, low


def matmul_t(left, right):
    return lax.dot_general(
        left, right, (((1,), (1,)), ((), ())), preferred_element_type=jnp.float32
    )


def matmul(left, right):
    return jnp.dot(left, right, preferred_element_type=jnp.float32)


def filter_spectrum(kernel, tables):
    high, low = tables
    count = kernel.shape[0]
    kernel_high, kernel_low = split_float(kernel)
    both = matmul_t(jnp.concatenate([kernel_high, kernel_low], axis=0), high)
    return both[:count] + both[count:] + matmul_t(kernel_high, low)


def dense_conv(signal, spectrum, tables):
    high, low = tables
    count, length = signal.shape
    own = matmul_t(signal, high) + matmul_t(signal, low)
    own_real, own_imag = own[:, :length], own[:, length:]
    real, imag = spectrum[:, :length], spectrum[:, length:]
    prod = jnp.concatenate(
        [own_real * real - own_imag * imag, own_real * imag + own_imag * real], axis=1
    )
    prod_high, prod_low = split_float(prod)
    both = matmul(jnp.concatenate([prod_high, prod_low], axis=0), high)
    return (both[:count] + both[count:] + matmul(prod_high, low)) * (1.0 / length)


MESH = pl.DeviceIdType.MESH


def project_kernel(
    planes,
    chips,
    branches,
    tokens,
    weights,
    out,
    gathered,
    features,
    packed,
    paired,
    partial,
    arrived,
    z_send,
    z_recv,
    f_send,
    f_recv,
    p_send,
    p_recv,
    w_send,
    w_recv,
    r_send,
    r_recv,
    own_sem,
):
    place = lax.axis_index("seq")
    plane = lax.axis_index("mp")
    chip, core = place // 2, lax.rem(place, 2)
    rows, depth = tokens.shape[0], weights.shape[0]
    width = weights.shape[1] // branches
    own = width // (2 * chips)
    sibling = (chip * 2 + 1 - core, plane)

    barrier = pltpu.get_barrier_semaphore()
    partners = [(place, lax.rem(plane + step, planes)) for step in range(1, planes)]
    partners += [(lax.rem(chip + step, chips) * 2 + core, plane) for step in range(1, chips)]
    partners += [sibling]
    for partner in partners:
        pl.semaphore_signal(barrier, inc=1, device_id=partner, device_id_type=MESH)
    pl.semaphore_wait(barrier, len(partners))

    def remote(source, target, send, recv, device):
        return pltpu.make_async_remote_copy(
            src_ref=source,
            dst_ref=target,
            send_sem=send,
            recv_sem=recv,
            device_id=device,
            device_id_type=MESH,
        )

    z_copies = []
    for step in range(1, planes):
        copy = remote(
            tokens,
            gathered.at[plane],
            z_send.at[step],
            z_recv.at[plane],
            (place, lax.rem(plane + step, planes)),
        )
        copy.start()
        z_copies.append(copy)
    gathered[plane] = tokens[...]

    def scatter(step):
        slot = lax.rem(plane - step + planes, planes)
        if step:
            remote(
                tokens, gathered.at[slot], z_send.at[step], z_recv.at[slot], (place, slot)
            ).wait_recv()

        @pl.when(slot == chip)
        def _():
            pltpu.make_async_copy(gathered.at[slot], features.at[place], own_sem).start()

        @pl.when(slot != chip)
        def _():
            remote(
                gathered.at[slot],
                features.at[place],
                f_send.at[step],
                f_recv.at[chip],
                (slot * 2 + core, plane),
            ).start()

    scatter(0)

    for branch in range(branches):
        turned = weights[:, branch * width : (branch + 1) * width].T
        for group in range(2 * chips):
            packed[group % 2, group // 2, branch * own : (branch + 1) * own, :] = turned[
                group * own : (group + 1) * own
            ]
    w_copy = remote(packed.at[1 - core], paired, w_send, w_recv, sibling)
    w_copy.start()

    for step in range(1, planes):
        scatter(step)

    p_copies = []
    for step in range(chips):
        source = lax.rem(chip + step, chips)
        piece = features.at[source * 2 + core]
        if step == 0:
            pltpu.make_async_copy(gathered.at[chip], piece, own_sem).wait()
        else:
            remote(
                gathered.at[0], piece, f_send.at[0], f_recv.at[source], (source * 2 + core, plane)
            ).wait_recv()
        copy = remote(piece, piece, p_send.at[step], p_recv.at[source], sibling)
        copy.start()
        p_copies.append(copy)
    w_copy.wait_recv()
    for step in range(chips):
        source = lax.rem(chip + step, chips)
        piece = features.at[source * 2 + 1 - core]
        remote(piece, piece, p_send.at[step], p_recv.at[source], sibling).wait_recv()

    here = pl.ds(pl.multiple_of(core * depth, depth), depth)
    there = pl.ds(pl.multiple_of((1 - core) * depth, depth), depth)
    span = 2

    def product(target, block):
        near = features[pl.ds(block * span, span), :, here].reshape(span * rows, depth)
        far = features[pl.ds(block * span, span), :, there].reshape(span * rows, depth)
        return matmul_t(packed[core, target], near) + matmul_t(paired[target], far)

    blocks = 2 * chips // span
    r_copies = []
    for step in list(range(1, chips)):
        target = lax.rem(chip + step, chips)

        def fill(block, carry, target=target, step=step):
            columns = pl.ds(pl.multiple_of(block * span * rows, span * rows), span * rows)
            partial[step - 1, :, columns] = product(target, block).astype(jnp.bfloat16)
            return carry

        lax.fori_loop(0, blocks, fill, 0)
        copy = remote(
            partial.at[step - 1],
            arrived.at[step - 1],
            r_send.at[step - 1],
            r_recv.at[step - 1],
            (target * 2 + core, plane),
        )
        copy.start()
        r_copies.append(copy)

    def mine(block, carry):
        columns = pl.ds(pl.multiple_of(block * span * rows, span * rows), span * rows)
        total[:, columns] = product(chip, block)
        return carry

    total = out[1]
    lax.fori_loop(0, blocks, mine, 0)
    for copy in r_copies:
        copy.wait_recv()

    def add(block, carry):
        columns = pl.ds(pl.multiple_of(block * span * rows, span * rows), span * rows)
        value = total[:, columns]
        for step in range(chips - 1):
            value = value + arrived[step, :, columns].astype(jnp.float32)
        out[0][:, columns] = value.astype(jnp.bfloat16)
        return carry

    lax.fori_loop(0, blocks, add, 0)

    for copy in z_copies + p_copies + [w_copy] + r_copies:
        copy.wait_send()
    for step in range(planes):
        slot = lax.rem(plane - step + planes, planes)

        @pl.when(slot != chip)
        def _():
            remote(
                gathered.at[slot],
                features.at[place],
                f_send.at[step],
                f_recv.at[chip],
                (slot * 2 + core, plane),
            ).wait_send()


def projected_channels(tokens, w_proj):
    depth, branches, width = w_proj.shape
    rows, wide = tokens.shape
    groups, planes = lax.axis_size("seq"), lax.axis_size("mp")
    chips = groups // 2
    own = width // groups
    length = rows * groups
    dma = pltpu.SemaphoreType.DMA

    def body(tokens_ref, weights_ref, out_ref, total_ref, *rest):
        project_kernel(planes, chips, branches, tokens_ref, weights_ref, (out_ref, total_ref), *rest)

    vmem = pl.BlockSpec(memory_space=pltpu.VMEM)
    half = jnp.bfloat16
    return pl.pallas_call(
        body,
        out_shape=jax.ShapeDtypeStruct((branches * own, length), half),
        in_specs=[vmem, vmem],
        out_specs=vmem,
        scratch_shapes=[
            pltpu.VMEM((branches * own, length), jnp.float32),
            pltpu.VMEM((planes, rows, wide), half),
            pltpu.VMEM((groups, rows, wide), half),
            pltpu.VMEM((2, chips, branches * own, depth), half),
            pltpu.VMEM((chips, branches * own, depth), half),
            pltpu.VMEM((chips - 1, branches * own, length), half),
            pltpu.VMEM((chips - 1, branches * own, length), half),
            dma((planes,)),
            dma((planes,)),
            dma((planes,)),
            dma((chips,)),
            dma((chips,)),
            dma((chips,)),
            dma,
            dma,
            dma((chips - 1,)),
            dma((chips - 1,)),
            dma,
        ],
        compiler_params=pltpu.CompilerParams(
            collective_id=0, has_side_effects=True, vmem_limit_bytes=48 * 1024 * 1024
        ),
    )(tokens, w_proj.reshape(depth, branches * width))


def by_tokens(tokens, w_proj, short_filter, long_filter, skip_gain):
    depth, branches, width = w_proj.shape
    groups = lax.axis_size("seq")
    own = width // groups
    length = tokens.shape[0] * groups
    tables = tuple(jnp.asarray(part) for part in dft_tables(length))
    first = lax.axis_index("seq") * own
    taps = lax.dynamic_slice_in_dim(short_filter, first, own, axis=2)
    gain = lax.dynamic_slice_in_dim(skip_gain, first, own, axis=0)
    spectrum = filter_spectrum(long_filter, tables)
    projected = projected_channels(tokens, w_proj).reshape(branches, own, length)
    margin = short_filter.shape[1] - 1
    padded = jnp.pad(projected.astype(jnp.float32), ((0, 0), (0, 0), (margin, 0)))
    mixed = jnp.zeros((branches, own, length), jnp.float32)
    for offset in range(margin + 1):
        mixed = mixed + taps[:, offset, :, None] * padded[:, :, margin - offset : margin - offset + length]
    product = (mixed[1] * mixed[2]).astype(jnp.bfloat16)
    convolved = dense_conv(product, spectrum, tables).astype(jnp.bfloat16).astype(jnp.float32)
    result = mixed[0] * (convolved + gain[:, None] * product.astype(jnp.float32))
    returned = lax.all_to_all(
        result.astype(jnp.bfloat16), "seq", split_axis=1, concat_axis=0, tiled=True
    )
    return returned.T


def on_device(tokens, w_proj, short_filter, long_filter, skip_gain):
    chips = lax.axis_size("mp")
    paired = lax.axis_size("seq") == 2 * chips and tokens.shape[1] == 2 * w_proj.shape[0]
    if paired and tokens.shape[0] < w_proj.shape[0]:
        return by_tokens(tokens, w_proj, short_filter, long_filter, skip_gain)
    return by_weights(tokens, w_proj, short_filter, long_filter, skip_gain)


def solution(mesh):
    return jax.shard_map(
        on_device,
        mesh=mesh,
        in_specs=(
            P("seq", "mp"),
            P("seq", None, "mp"),
            P(None, None, "mp"),
            P(("mp", "seq"), None),
            P("mp"),
        ),
        out_specs=P("seq", "mp"),
        check_vma=False,
    )
```

```python
import functools
import math

import jax
import jax.numpy as jnp
import numpy as np
from jax import lax
from jax.experimental import pallas as pl
from jax.experimental.pallas import tpu as pltpu
from jax.sharding import PartitionSpec as P


def shifted(value, axis, steps):
    count = lax.axis_size(axis)
    leading, last = (max(0, -steps), min(count, count - steps))
    return lax.ppermute(value, axis, [(source, source + steps) for source in range(leading, last)])


def transform(real_part, imag_part, orient, filled):
    length = real_part.shape[-1]
    first = math.gcd(length, 64)
    highest = lax.Precision.HIGHEST
    if length <= 64 or first == 1:
        counter = jnp.arange(length, dtype=jnp.int32)
        angles = (
            2.0
            * math.pi
            / length
            * (counter[:, None] * counter[None, :] % length).astype(jnp.float32)
        )
        cosine = jnp.cos(angles)
        sine = jnp.sin(angles)
        new_real = jnp.dot(real_part, cosine, precision=highest) - orient * jnp.dot(
            imag_part, sine, precision=highest
        )
        new_imag = jnp.dot(imag_part, cosine, precision=highest) + orient * jnp.dot(
            real_part, sine, precision=highest
        )
        return (new_real, new_imag)
    second = length // first
    outer = real_part.shape[:-1]
    live = first
    if filled > 0 and filled % second == 0:
        live = filled // second
    real_grid = real_part.reshape(outer + (first, second))[..., :live, :]
    imag_grid = imag_part.reshape(outer + (first, second))[..., :live, :]
    counter = jnp.arange(first, dtype=jnp.int32)
    angles = (
        2.0 * math.pi / first * (counter[:, None] * counter[None, :] % first).astype(jnp.float32)
    )
    cosine = jnp.cos(angles)[:live]
    sine = jnp.sin(angles)[:live]
    section_real = jnp.einsum(
        "...ab,ak->...kb", real_grid, cosine, precision=highest
    ) - orient * jnp.einsum("...ab,ak->...kb", imag_grid, sine, precision=highest)
    section_imag = jnp.einsum(
        "...ab,ak->...kb", imag_grid, cosine, precision=highest
    ) + orient * jnp.einsum("...ab,ak->...kb", real_grid, sine, precision=highest)
    freq_rows = jnp.arange(first, dtype=jnp.int32)[:, None]
    time_cols = jnp.arange(second, dtype=jnp.int32)[None, :]
    twiddle = 2.0 * math.pi / length * (freq_rows * time_cols).astype(jnp.float32)
    twist_cos = jnp.cos(twiddle)
    twist_sin = jnp.sin(twiddle)
    turned_real = section_real * twist_cos - orient * section_imag * twist_sin
    turned_imag = section_imag * twist_cos + orient * section_real * twist_sin
    inner_real, inner_imag = transform(turned_real, turned_imag, orient, 0)
    final_real = jnp.swapaxes(inner_real, -1, -2).reshape(outer + (length,))
    final_imag = jnp.swapaxes(inner_imag, -1, -2).reshape(outer + (length,))
    return (final_real, final_imag)


def mirrored(values):
    return jnp.concatenate([values[:, :1], values[:, :0:-1]], axis=1)


def long_conv(signal, kernel):
    seq_len = signal.shape[-1]
    padded_signal = jnp.pad(signal.astype(jnp.float32), ((0, 0), (0, seq_len)))
    padded_kernel = jnp.pad(kernel, ((0, 0), (0, seq_len)))
    joint_real, joint_imag = transform(padded_signal, padded_kernel, -1.0, seq_len)
    mirror_real = mirrored(joint_real)
    mirror_imag = mirrored(joint_imag)
    signal_real = 0.5 * (joint_real + mirror_real)
    signal_imag = 0.5 * (joint_imag - mirror_imag)
    kernel_real = 0.5 * (joint_imag + mirror_imag)
    kernel_imag = -0.5 * (joint_real - mirror_real)
    prod_real = signal_real * kernel_real - signal_imag * kernel_imag
    prod_imag = signal_real * kernel_imag + signal_imag * kernel_real
    back_real, back_imag = transform(prod_real, prod_imag, 1.0, 0)
    return back_real[:, :seq_len] / (2.0 * seq_len)


def by_weights(tokens, w_proj, short_filter, long_filter, skip_gain):
    rows_dev = tokens.shape[0]
    margin = short_filter.shape[1] - 1
    width = w_proj.shape[2]
    source = lax.all_gather(tokens, "mp", axis=1, tiled=True)
    projected = jnp.einsum(
        "td,dpc->tpc",
        source,
        lax.all_gather(w_proj, "seq", axis=0, tiled=True),
        preferred_element_type=jnp.float32,
    ).astype(jnp.bfloat16)
    tail = shifted(projected[rows_dev - margin :], "seq", 1)
    extended = jnp.concatenate([tail, projected], axis=0).astype(jnp.float32)
    mixed = jnp.zeros((rows_dev, 3, width), jnp.float32)
    for offset in range(margin + 1):
        mixed = (
            mixed
            + short_filter[:, offset, :][None]
            * extended[margin - offset : margin - offset + rows_dev]
        )
    query_rows = mixed[:, 0]
    product = (mixed[:, 1] * mixed[:, 2]).astype(jnp.bfloat16)
    groups = lax.axis_size("seq")
    channel_count = width // groups
    outgoing = product.reshape(rows_dev, groups, channel_count).transpose(1, 2, 0)
    arrived = lax.all_to_all(outgoing, "seq", split_axis=0, concat_axis=2, tiled=True)[0]
    convolved = long_conv(arrived, long_filter).astype(jnp.bfloat16)[None]
    returned = lax.all_to_all(convolved, "seq", split_axis=2, concat_axis=0, tiled=True)
    back_rows = returned.transpose(2, 0, 1).reshape(rows_dev, width)
    result = query_rows * (
        back_rows.astype(jnp.float32) + skip_gain[None, :] * product.astype(jnp.float32)
    )
    return result.astype(jnp.bfloat16)


def split_float(value):
    high = value.astype(jnp.bfloat16)
    low = (value - high.astype(jnp.float32)).astype(jnp.bfloat16)
    return high, low


def dft_tables(length):
    phase = (4 * np.arange(length)[:, None] + 1) * np.arange(length)[None, :] % (4 * length)
    angles = phase * (2.0 * np.pi / (4 * length))
    table = np.concatenate([np.cos(angles), np.sin(angles)], axis=0).astype(np.float32)
    high = table.astype(jnp.bfloat16)
    low = (table - high.astype(np.float32)).astype(jnp.bfloat16)
    return high, low


def matmul_t(left, right):
    return lax.dot_general(
        left, right, (((1,), (1,)), ((), ())), preferred_element_type=jnp.float32
    )


def matmul(left, right):
    return jnp.dot(left, right, preferred_element_type=jnp.float32)


def filter_spectrum(kernel, tables):
    high, low = tables
    count = kernel.shape[0]
    kernel_high, kernel_low = split_float(kernel)
    both = matmul_t(jnp.concatenate([kernel_high, kernel_low], axis=0), high)
    return both[:count] + both[count:] + matmul_t(kernel_high, low)


def dense_conv(signal, spectrum, tables):
    high, low = tables
    count, length = signal.shape
    own = matmul_t(signal, high) + matmul_t(signal, low)
    own_real, own_imag = own[:, :length], own[:, length:]
    real, imag = spectrum[:, :length], spectrum[:, length:]
    prod = jnp.concatenate(
        [own_real * real - own_imag * imag, own_real * imag + own_imag * real], axis=1
    )
    prod_high, prod_low = split_float(prod)
    both = matmul(jnp.concatenate([prod_high, prod_low], axis=0), high)
    return (both[:count] + both[count:] + matmul(prod_high, low)) * (1.0 / length)


MESH = pl.DeviceIdType.MESH
PARTS = 2


def project_kernel(
    planes,
    chips,
    branches,
    tokens,
    weights,
    out,
    total,
    gathered,
    features,
    packed,
    paired,
    partial,
    arrived,
    z_send,
    z_recv,
    f_send,
    f_recv,
    p_send,
    p_recv,
    w_send,
    w_recv,
    r_send,
    r_recv,
    own_sem,
):
    place = lax.axis_index("seq")
    plane = lax.axis_index("mp")
    chip, core = place // 2, lax.rem(place, 2)
    rows, depth = tokens.shape[0], weights.shape[0]
    width = weights.shape[1] // branches
    own = width // (2 * chips)
    sibling = (chip * 2 + 1 - core, plane)

    barrier = pltpu.get_barrier_semaphore()
    partners = [(place, lax.rem(plane + step, planes)) for step in range(1, planes)]
    partners += [(lax.rem(chip + step, chips) * 2 + core, plane) for step in range(1, chips)]
    partners += [sibling]
    for partner in partners:
        pl.semaphore_signal(barrier, inc=1, device_id=partner, device_id_type=MESH)
    pl.semaphore_wait(barrier, len(partners))

    def remote(source, target, send, recv, device):
        return pltpu.make_async_remote_copy(
            src_ref=source,
            dst_ref=target,
            send_sem=send,
            recv_sem=recv,
            device_id=device,
            device_id_type=MESH,
        )

    share = rows // PARTS

    def cut(ref, part):
        return ref.at[part * share : (part + 1) * share]

    def along_z(part):
        copies = []
        for step in range(1, planes):
            copy = remote(
                cut(tokens, part),
                cut(gathered.at[plane], part),
                z_send.at[part, step],
                z_recv.at[part, plane],
                (place, lax.rem(plane + step, planes)),
            )
            copy.start()
            copies.append(copy)
        return copies

    z_copies = along_z(0)
    gathered[plane] = tokens[...]

    def scatter_copy(part, step):
        slot = lax.rem(plane - step + planes, planes)
        return slot, remote(
            cut(gathered.at[slot], part),
            cut(features.at[place], part),
            f_send.at[part, step],
            f_recv.at[part, chip],
            (slot * 2 + core, plane),
        )

    def own_copy(part):
        return pltpu.make_async_copy(
            cut(gathered.at[chip], part), cut(features.at[place], part), own_sem.at[part]
        )

    def scatter(part, step):
        slot, copy = scatter_copy(part, step)
        if step:
            remote(
                cut(tokens, part),
                cut(gathered.at[slot], part),
                z_send.at[part, step],
                z_recv.at[part, slot],
                (place, slot),
            ).wait_recv()

        @pl.when(slot == chip)
        def _():
            own_copy(part).start()

        @pl.when(slot != chip)
        def _():
            copy.start()

    for part in range(PARTS):
        scatter(part, 0)

    for branch in range(branches):
        turned = weights[:, branch * width : (branch + 1) * width].T
        for group in range(2 * chips):
            packed[group % 2, group // 2, branch * own : (branch + 1) * own, :] = turned[
                group * own : (group + 1) * own
            ]
    w_copy = remote(packed.at[1 - core], paired, w_send, w_recv, sibling)
    w_copy.start()
    for part in range(1, PARTS):
        for copy in z_copies[-(planes - 1) :]:
            copy.wait_send()
        z_copies += along_z(part)

    p_copies, r_copies = [], []
    here = pl.ds(pl.multiple_of(core * depth, depth), depth)
    there = pl.ds(pl.multiple_of((1 - core) * depth, depth), depth)

    def forward(part):
        for step in range(chips):
            source = lax.rem(chip + step, chips)
            piece = cut(features.at[source * 2 + core], part)
            if step == 0:
                own_copy(part).wait()
            else:
                remote(
                    cut(gathered.at[0], part),
                    piece,
                    f_send.at[part, 0],
                    f_recv.at[part, source],
                    (source * 2 + core, plane),
                ).wait_recv()
            copy = remote(piece, piece, p_send.at[part, step], p_recv.at[part, source], sibling)
            copy.start()
            p_copies.append(copy)

    span = 2 * chips // 2
    across = span * share

    def push(part):
        if part == 0:
            w_copy.wait_recv()
        for step in range(chips):
            source = lax.rem(chip + step, chips)
            piece = cut(features.at[source * 2 + 1 - core], part)
            remote(piece, piece, p_send.at[part, step], p_recv.at[part, source], sibling).wait_recv()

        def product(target, block):
            which = (pl.ds(block * span, span), slice(part * share, (part + 1) * share))
            near = features[(*which, here)].reshape(across, depth)
            far = features[(*which, there)].reshape(across, depth)
            return matmul_t(packed[core, target], near) + matmul_t(paired[target], far)

        for step in list(range(1, chips)) + [0]:
            target = lax.rem(chip + step, chips)

            def fill(block, carry, target=target, step=step):
                columns = pl.ds(pl.multiple_of(block * across, across), across)
                value = product(target, block)
                if step:
                    partial[part, step - 1, :, columns] = value.astype(jnp.bfloat16)
                else:
                    total[part, :, columns] = value
                return carry

            lax.fori_loop(0, 2, fill, 0)
            if step:
                copy = remote(
                    partial.at[part, step - 1],
                    arrived.at[part, step - 1],
                    r_send.at[part, step - 1],
                    r_recv.at[part, step - 1],
                    (target * 2 + core, plane),
                )
                copy.start()
                r_copies.append(copy)

    for step in range(1, planes):
        scatter(0, step)
    forward(0)
    for part in range(PARTS):
        if part + 1 < PARTS:
            for step in range(1, planes):
                scatter(part + 1, step)
        push(part)
        if part + 1 < PARTS:
            forward(part + 1)

    for copy in r_copies:
        copy.wait_recv()

    low = lax.broadcasted_iota(jnp.int32, (out.shape[0], rows), 1) < share

    def add(pair, carry):
        columns = pl.ds(pl.multiple_of(pair * rows, rows), rows)
        values = []
        for part in range(PARTS):
            value = total[part, :, columns]
            for step in range(chips - 1):
                value = value + arrived[part, step, :, columns].astype(jnp.float32)
            values.append(value)
        first = jnp.where(low, values[0], pltpu.roll(values[1], share, 1))
        second = jnp.where(low, pltpu.roll(values[0], share, 1), values[1])
        at = pl.multiple_of(pair * 2 * rows, 2 * rows)
        out[:, pl.ds(at, rows)] = first.astype(jnp.bfloat16)
        out[:, pl.ds(pl.multiple_of(at + rows, rows), rows)] = second.astype(jnp.bfloat16)
        return carry

    lax.fori_loop(0, chips, add, 0)

    for copy in z_copies[-(planes - 1) :] + p_copies + [w_copy] + r_copies:
        copy.wait_send()
    for part in range(PARTS):
        for step in range(planes):
            slot, copy = scatter_copy(part, step)

            @pl.when(slot != chip)
            def _(copy=copy):
                copy.wait_send()


def projected_channels(tokens, w_proj):
    depth, branches, width = w_proj.shape
    rows, wide = tokens.shape
    groups, planes = lax.axis_size("seq"), lax.axis_size("mp")
    chips = groups // 2
    own = width // groups
    length = rows * groups
    dma = pltpu.SemaphoreType.DMA

    vmem = pl.BlockSpec(memory_space=pltpu.VMEM)
    half = jnp.bfloat16
    return pl.pallas_call(
        functools.partial(project_kernel, planes, chips, branches),
        out_shape=jax.ShapeDtypeStruct((branches * own, length), half),
        in_specs=[vmem, vmem],
        out_specs=vmem,
        scratch_shapes=[
            pltpu.VMEM((PARTS, branches * own, length // PARTS), jnp.float32),
            pltpu.VMEM((planes, rows, wide), half),
            pltpu.VMEM((groups, rows, wide), half),
            pltpu.VMEM((2, chips, branches * own, depth), half),
            pltpu.VMEM((chips, branches * own, depth), half),
            pltpu.VMEM((PARTS, chips - 1, branches * own, length // PARTS), half),
            pltpu.VMEM((PARTS, chips - 1, branches * own, length // PARTS), half),
            dma((PARTS, planes)),
            dma((PARTS, planes)),
            dma((PARTS, planes)),
            dma((PARTS, chips)),
            dma((PARTS, chips)),
            dma((PARTS, chips)),
            dma,
            dma,
            dma((PARTS, chips - 1)),
            dma((PARTS, chips - 1)),
            dma((PARTS,)),
        ],
        compiler_params=pltpu.CompilerParams(
            collective_id=0, has_side_effects=True, vmem_limit_bytes=48 * 1024 * 1024
        ),
    )(tokens, w_proj.reshape(depth, branches * width))


def by_tokens(tokens, w_proj, short_filter, long_filter, skip_gain):
    depth, branches, width = w_proj.shape
    groups = lax.axis_size("seq")
    own = width // groups
    length = tokens.shape[0] * groups
    tables = tuple(jnp.asarray(part) for part in dft_tables(length))
    first = lax.axis_index("seq") * own
    taps = lax.dynamic_slice_in_dim(short_filter, first, own, axis=2)
    gain = lax.dynamic_slice_in_dim(skip_gain, first, own, axis=0)
    spectrum = filter_spectrum(long_filter, tables)
    projected = projected_channels(tokens, w_proj).reshape(branches, own, length)
    margin = short_filter.shape[1] - 1
    padded = jnp.pad(projected.astype(jnp.float32), ((0, 0), (0, 0), (margin, 0)))
    mixed = jnp.zeros((branches, own, length), jnp.float32)
    for offset in range(margin + 1):
        mixed = mixed + taps[:, offset, :, None] * padded[:, :, margin - offset : margin - offset + length]
    product = (mixed[1] * mixed[2]).astype(jnp.bfloat16)
    convolved = dense_conv(product, spectrum, tables).astype(jnp.bfloat16).astype(jnp.float32)
    result = mixed[0] * (convolved + gain[:, None] * product.astype(jnp.float32))
    returned = lax.all_to_all(
        result.astype(jnp.bfloat16), "seq", split_axis=1, concat_axis=0, tiled=True
    )
    return returned.T


def on_device(tokens, w_proj, short_filter, long_filter, skip_gain):
    chips = lax.axis_size("mp")
    paired = lax.axis_size("seq") == 2 * chips and tokens.shape[1] == 2 * w_proj.shape[0]
    if paired and tokens.shape[0] < w_proj.shape[0]:
        return by_tokens(tokens, w_proj, short_filter, long_filter, skip_gain)
    return by_weights(tokens, w_proj, short_filter, long_filter, skip_gain)


def solution(mesh):
    return jax.shard_map(
        on_device,
        mesh=mesh,
        in_specs=(
            P("seq", "mp"),
            P("seq", None, "mp"),
            P(None, None, "mp"),
            P(("mp", "seq"), None),
            P("mp"),
        ),
        out_specs=P("seq", "mp"),
        check_vma=False,
    )
```

```python
import functools
import math

import jax
import jax.numpy as jnp
import numpy as np
from jax import lax
from jax.experimental import pallas as pl
from jax.experimental.pallas import tpu as pltpu
from jax.sharding import PartitionSpec as P


def shifted(value, axis, steps):
    count = lax.axis_size(axis)
    leading, last = (max(0, -steps), min(count, count - steps))
    return lax.ppermute(value, axis, [(source, source + steps) for source in range(leading, last)])


def transform(real_part, imag_part, orient, filled):
    length = real_part.shape[-1]
    first = math.gcd(length, 64)
    highest = lax.Precision.HIGHEST
    if length <= 64 or first == 1:
        counter = jnp.arange(length, dtype=jnp.int32)
        angles = (
            2.0
            * math.pi
            / length
            * (counter[:, None] * counter[None, :] % length).astype(jnp.float32)
        )
        cosine = jnp.cos(angles)
        sine = jnp.sin(angles)
        new_real = jnp.dot(real_part, cosine, precision=highest) - orient * jnp.dot(
            imag_part, sine, precision=highest
        )
        new_imag = jnp.dot(imag_part, cosine, precision=highest) + orient * jnp.dot(
            real_part, sine, precision=highest
        )
        return (new_real, new_imag)
    second = length // first
    outer = real_part.shape[:-1]
    live = first
    if filled > 0 and filled % second == 0:
        live = filled // second
    real_grid = real_part.reshape(outer + (first, second))[..., :live, :]
    imag_grid = imag_part.reshape(outer + (first, second))[..., :live, :]
    counter = jnp.arange(first, dtype=jnp.int32)
    angles = (
        2.0 * math.pi / first * (counter[:, None] * counter[None, :] % first).astype(jnp.float32)
    )
    cosine = jnp.cos(angles)[:live]
    sine = jnp.sin(angles)[:live]
    section_real = jnp.einsum(
        "...ab,ak->...kb", real_grid, cosine, precision=highest
    ) - orient * jnp.einsum("...ab,ak->...kb", imag_grid, sine, precision=highest)
    section_imag = jnp.einsum(
        "...ab,ak->...kb", imag_grid, cosine, precision=highest
    ) + orient * jnp.einsum("...ab,ak->...kb", real_grid, sine, precision=highest)
    freq_rows = jnp.arange(first, dtype=jnp.int32)[:, None]
    time_cols = jnp.arange(second, dtype=jnp.int32)[None, :]
    twiddle = 2.0 * math.pi / length * (freq_rows * time_cols).astype(jnp.float32)
    twist_cos = jnp.cos(twiddle)
    twist_sin = jnp.sin(twiddle)
    turned_real = section_real * twist_cos - orient * section_imag * twist_sin
    turned_imag = section_imag * twist_cos + orient * section_real * twist_sin
    inner_real, inner_imag = transform(turned_real, turned_imag, orient, 0)
    final_real = jnp.swapaxes(inner_real, -1, -2).reshape(outer + (length,))
    final_imag = jnp.swapaxes(inner_imag, -1, -2).reshape(outer + (length,))
    return (final_real, final_imag)


def mirrored(values):
    return jnp.concatenate([values[:, :1], values[:, :0:-1]], axis=1)


def long_conv(signal, kernel):
    seq_len = signal.shape[-1]
    padded_signal = jnp.pad(signal.astype(jnp.float32), ((0, 0), (0, seq_len)))
    padded_kernel = jnp.pad(kernel, ((0, 0), (0, seq_len)))
    joint_real, joint_imag = transform(padded_signal, padded_kernel, -1.0, seq_len)
    mirror_real = mirrored(joint_real)
    mirror_imag = mirrored(joint_imag)
    signal_real = 0.5 * (joint_real + mirror_real)
    signal_imag = 0.5 * (joint_imag - mirror_imag)
    kernel_real = 0.5 * (joint_imag + mirror_imag)
    kernel_imag = -0.5 * (joint_real - mirror_real)
    prod_real = signal_real * kernel_real - signal_imag * kernel_imag
    prod_imag = signal_real * kernel_imag + signal_imag * kernel_real
    back_real, back_imag = transform(prod_real, prod_imag, 1.0, 0)
    return back_real[:, :seq_len] / (2.0 * seq_len)


def by_weights(tokens, w_proj, short_filter, long_filter, skip_gain):
    rows_dev = tokens.shape[0]
    margin = short_filter.shape[1] - 1
    width = w_proj.shape[2]
    source = lax.all_gather(tokens, "mp", axis=1, tiled=True)
    projected = jnp.einsum(
        "td,dpc->tpc",
        source,
        lax.all_gather(w_proj, "seq", axis=0, tiled=True),
        preferred_element_type=jnp.float32,
    ).astype(jnp.bfloat16)
    tail = shifted(projected[rows_dev - margin :], "seq", 1)
    extended = jnp.concatenate([tail, projected], axis=0).astype(jnp.float32)
    mixed = jnp.zeros((rows_dev, 3, width), jnp.float32)
    for offset in range(margin + 1):
        mixed = (
            mixed
            + short_filter[:, offset, :][None]
            * extended[margin - offset : margin - offset + rows_dev]
        )
    query_rows = mixed[:, 0]
    product = (mixed[:, 1] * mixed[:, 2]).astype(jnp.bfloat16)
    groups = lax.axis_size("seq")
    channel_count = width // groups
    outgoing = product.reshape(rows_dev, groups, channel_count).transpose(1, 2, 0)
    arrived = lax.all_to_all(outgoing, "seq", split_axis=0, concat_axis=2, tiled=True)[0]
    convolved = long_conv(arrived, long_filter).astype(jnp.bfloat16)[None]
    returned = lax.all_to_all(convolved, "seq", split_axis=2, concat_axis=0, tiled=True)
    back_rows = returned.transpose(2, 0, 1).reshape(rows_dev, width)
    result = query_rows * (
        back_rows.astype(jnp.float32) + skip_gain[None, :] * product.astype(jnp.float32)
    )
    return result.astype(jnp.bfloat16)


def split_float(value):
    high = value.astype(jnp.bfloat16)
    low = (value - high.astype(jnp.float32)).astype(jnp.bfloat16)
    return high, low


def dft_tables(length):
    phase = (4 * np.arange(length)[:, None] + 1) * np.arange(length)[None, :] % (4 * length)
    angles = phase * (2.0 * np.pi / (4 * length))
    table = np.concatenate([np.cos(angles), np.sin(angles)], axis=0).astype(np.float32)
    high = table.astype(jnp.bfloat16)
    low = (table - high.astype(np.float32)).astype(jnp.bfloat16)
    return high, low


def matmul_t(left, right):
    return lax.dot_general(
        left, right, (((1,), (1,)), ((), ())), preferred_element_type=jnp.float32
    )


def matmul(left, right):
    return jnp.dot(left, right, preferred_element_type=jnp.float32)


MESH = pl.DeviceIdType.MESH
PARTS = 2


def project_kernel(
    planes,
    chips,
    branches,
    tokens,
    weights,
    scalars,
    kernel,
    high_table,
    low_table,
    out,
    high,
    low,
    spectrum,
    projected,
    spectral,
    leaving,
    collected,
    t_sem,
    a_send,
    a_recv,
    total,
    gathered,
    features,
    packed,
    paired,
    partial,
    arrived,
    z_send,
    z_recv,
    f_send,
    f_recv,
    p_send,
    p_recv,
    w_send,
    w_recv,
    r_send,
    r_recv,
    own_sem,
):
    place = lax.axis_index("seq")
    plane = lax.axis_index("mp")
    chip, core = place // 2, lax.rem(place, 2)
    rows, depth = tokens.shape[0], weights.shape[0]
    width = weights.shape[1] // branches
    own = width // (2 * chips)
    sibling = (chip * 2 + 1 - core, plane)

    barrier = pltpu.get_barrier_semaphore()
    partners = [(place, lax.rem(plane + step, planes)) for step in range(1, planes)]
    partners += [(lax.rem(chip + step, chips) * 2 + core, plane) for step in range(1, chips)]
    partners += [(lax.rem(chip + step, chips) * 2 + 1 - core, plane) for step in range(chips)]
    for partner in partners:
        pl.semaphore_signal(barrier, inc=1, device_id=partner, device_id_type=MESH)
    pl.semaphore_wait(barrier, len(partners))

    def remote(source, target, send, recv, device):
        return pltpu.make_async_remote_copy(
            src_ref=source,
            dst_ref=target,
            send_sem=send,
            recv_sem=recv,
            device_id=device,
            device_id_type=MESH,
        )

    share = rows // PARTS
    table_copies = [
        pltpu.make_async_copy(high_table, high, t_sem.at[0]),
        pltpu.make_async_copy(low_table, low, t_sem.at[1]),
    ]

    def cut(ref, part):
        return ref.at[part * share : (part + 1) * share]

    def along_z(part):
        copies = []
        for step in range(1, planes):
            copy = remote(
                cut(tokens, part),
                cut(gathered.at[plane], part),
                z_send.at[part, step],
                z_recv.at[part, plane],
                (place, lax.rem(plane + step, planes)),
            )
            copy.start()
            copies.append(copy)
        return copies

    z_copies = along_z(0)
    for copy in table_copies:
        copy.start()
    gathered[plane] = tokens[...]

    def scatter_copy(part, step):
        slot = lax.rem(plane - step + planes, planes)
        return slot, remote(
            cut(gathered.at[slot], part),
            cut(features.at[place], part),
            f_send.at[part, step],
            f_recv.at[part, chip],
            (slot * 2 + core, plane),
        )

    def own_copy(part):
        return pltpu.make_async_copy(
            cut(gathered.at[chip], part), cut(features.at[place], part), own_sem.at[part]
        )

    def scatter(part, step):
        slot, copy = scatter_copy(part, step)
        if step:
            remote(
                cut(tokens, part),
                cut(gathered.at[slot], part),
                z_send.at[part, step],
                z_recv.at[part, slot],
                (place, slot),
            ).wait_recv()

        @pl.when(slot == chip)
        def _():
            own_copy(part).start()

        @pl.when(slot != chip)
        def _():
            copy.start()

    for part in range(PARTS):
        scatter(part, 0)

    for branch in range(branches):
        turned = weights[:, branch * width : (branch + 1) * width].T
        for group in range(2 * chips):
            packed[group % 2, group // 2, branch * own : (branch + 1) * own, :] = turned[
                group * own : (group + 1) * own
            ]
    w_copy = remote(packed.at[1 - core], paired, w_send, w_recv, sibling)
    w_copy.start()
    for part in range(1, PARTS):
        for copy in z_copies[-(planes - 1) :]:
            copy.wait_send()
        z_copies += along_z(part)

    for copy in table_copies:
        copy.wait()
    length = kernel.shape[1]
    chunk = 2 * rows
    kernel_high, kernel_low = split_float(kernel[...])
    kernel_both = jnp.concatenate([kernel_high, kernel_low], axis=0)

    def transform_filter(block, carry):
        at = pl.ds(pl.multiple_of(block * chunk, chunk), chunk)
        both = matmul_t(kernel_both, high[at, :])
        spectrum[:, at] = both[:own] + both[own:] + matmul_t(kernel_high, low[at, :])
        return carry

    lax.fori_loop(0, 2 * length // chunk, transform_filter, 0)

    p_copies, r_copies = [], []
    here = pl.ds(pl.multiple_of(core * depth, depth), depth)
    there = pl.ds(pl.multiple_of((1 - core) * depth, depth), depth)

    def forward(part):
        for step in range(chips):
            source = lax.rem(chip + step, chips)
            piece = cut(features.at[source * 2 + core], part)
            if step == 0:
                own_copy(part).wait()
            else:
                remote(
                    cut(gathered.at[0], part),
                    piece,
                    f_send.at[part, 0],
                    f_recv.at[part, source],
                    (source * 2 + core, plane),
                ).wait_recv()
            copy = remote(piece, piece, p_send.at[part, step], p_recv.at[part, source], sibling)
            copy.start()
            p_copies.append(copy)

    span = 2 * chips // 2
    across = span * share

    def push(part):
        if part == 0:
            w_copy.wait_recv()
        for step in range(chips):
            source = lax.rem(chip + step, chips)
            piece = cut(features.at[source * 2 + 1 - core], part)
            remote(piece, piece, p_send.at[part, step], p_recv.at[part, source], sibling).wait_recv()

        def product(target, block):
            which = (pl.ds(block * span, span), slice(part * share, (part + 1) * share))
            near = features[(*which, here)].reshape(across, depth)
            far = features[(*which, there)].reshape(across, depth)
            return matmul_t(packed[core, target], near) + matmul_t(paired[target], far)

        for step in list(range(1, chips)) + [0]:
            target = lax.rem(chip + step, chips)

            def fill(block, carry, target=target, step=step):
                columns = pl.ds(pl.multiple_of(block * across, across), across)
                value = product(target, block)
                if step:
                    partial[part, step - 1, :, columns] = value.astype(jnp.bfloat16)
                else:
                    total[part, :, columns] = value
                return carry

            lax.fori_loop(0, 2, fill, 0)
            if step:
                copy = remote(
                    partial.at[part, step - 1],
                    arrived.at[part, step - 1],
                    r_send.at[part, step - 1],
                    r_recv.at[part, step - 1],
                    (target * 2 + core, plane),
                )
                copy.start()
                r_copies.append(copy)

    for step in range(1, planes):
        scatter(0, step)
    forward(0)
    for part in range(PARTS):
        if part + 1 < PARTS:
            for step in range(1, planes):
                scatter(part + 1, step)
        push(part)
        if part + 1 < PARTS:
            forward(part + 1)

    for copy in r_copies:
        copy.wait_recv()

    left = lax.broadcasted_iota(jnp.int32, (branches * own, rows), 1) < share

    def add(pair, carry):
        columns = pl.ds(pl.multiple_of(pair * rows, rows), rows)
        values = []
        for part in range(PARTS):
            value = total[part, :, columns]
            for step in range(chips - 1):
                value = value + arrived[part, step, :, columns].astype(jnp.float32)
            values.append(value)
        first = jnp.where(left, values[0], pltpu.roll(values[1], share, 1))
        second = jnp.where(left, pltpu.roll(values[0], share, 1), values[1])
        at = pl.multiple_of(pair * 2 * rows, 2 * rows)
        near, far = pl.ds(at, rows), pl.ds(pl.multiple_of(at + rows, rows), rows)
        projected[:, near] = first.astype(jnp.bfloat16).astype(jnp.float32)
        projected[:, far] = second.astype(jnp.bfloat16).astype(jnp.float32)
        return carry

    lax.fori_loop(0, chips, add, 0)

    token = lax.broadcasted_iota(jnp.int32, (own, length), 1)
    mixed = []
    for branch in range(branches):
        at = slice(branch * own, (branch + 1) * own)
        value = projected[at, :]
        result = scalars[at, 0:1] * value
        for offset in range(1, scalars.shape[1] - 1):
            moved = jnp.where(token >= offset, pltpu.roll(value, offset, 1), 0.0)
            result = result + scalars[at, offset : offset + 1] * moved
        mixed.append(result)
    signal = (mixed[1] * mixed[2]).astype(jnp.bfloat16)
    gain = scalars[0:own, scalars.shape[1] - 1 :]
    projected[0:own, :] = mixed[0]
    projected[own : 2 * own, :] = gain * signal.astype(jnp.float32)

    for block in range(length // chunk):
        real_at = slice(block * chunk, (block + 1) * chunk)
        imag_at = slice(length + block * chunk, length + (block + 1) * chunk)
        own_real = matmul_t(signal, high[real_at, :]) + matmul_t(signal, low[real_at, :])
        own_imag = matmul_t(signal, high[imag_at, :]) + matmul_t(signal, low[imag_at, :])
        real, imag = spectrum[:, real_at], spectrum[:, imag_at]
        for at, value in (
            (real_at, own_real * real - own_imag * imag),
            (imag_at, own_real * imag + own_imag * real),
        ):
            value_high, value_low = split_float(value)
            spectral[0:own, at] = value_high
            spectral[own : 2 * own, at] = value_low

    a_copies = []
    for step in list(range(1, chips)) + [0]:
        target = lax.rem(chip + step, chips)
        at = pl.ds(pl.multiple_of(target * chunk, chunk), chunk)
        both = matmul(spectral[...], high[:, at])
        value = both[:own] + both[own:] + matmul(spectral[0:own, :], low[:, at])
        value = (value * (1.0 / length)).astype(jnp.bfloat16).astype(jnp.float32)
        value = (projected[0:own, at] * (value + projected[own : 2 * own, at])).astype(jnp.bfloat16)
        leaving[step, 0] = value[:, :rows]
        leaving[step, 1] = value[:, rows:]
        for other in (1, 0):
            side = core if other == 0 else 1 - core
            if step == 0 and other == 0:
                collected[place] = leaving[step, side]
                continue
            copy = remote(
                leaving.at[step, side],
                collected.at[place],
                a_send.at[step, other],
                a_recv.at[place],
                (target * 2 + side, plane),
            )
            copy.start()
            a_copies.append(copy)
    for step in range(1, 2 * chips):
        source = lax.rem(place + step, 2 * chips)
        remote(
            leaving.at[0, 0], collected.at[source], a_send.at[0, 0], a_recv.at[source], (source, plane)
        ).wait_recv()
    out[...] = collected[...].reshape(2 * chips * own, rows).T

    for copy in z_copies[-(planes - 1) :] + p_copies + [w_copy] + r_copies + a_copies:
        copy.wait_send()
    for part in range(PARTS):
        for step in range(planes):
            slot, copy = scatter_copy(part, step)

            @pl.when(slot != chip)
            def _(copy=copy):
                copy.wait_send()


def operator_kernel(tokens, w_proj, scalars, long_filter, tables):
    depth, branches, width = w_proj.shape
    rows, wide = tokens.shape
    groups, planes = lax.axis_size("seq"), lax.axis_size("mp")
    chips = groups // 2
    own = width // groups
    length = rows * groups
    dma = pltpu.SemaphoreType.DMA

    vmem = pl.BlockSpec(memory_space=pltpu.VMEM)
    half = jnp.bfloat16
    return pl.pallas_call(
        functools.partial(project_kernel, planes, chips, branches),
        out_shape=jax.ShapeDtypeStruct((rows, width), half),
        in_specs=[vmem] * 4 + [pl.BlockSpec(memory_space=pl.ANY)] * 2,
        out_specs=vmem,
        scratch_shapes=[
            pltpu.VMEM((2 * length, length), half),
            pltpu.VMEM((2 * length, length), half),
            pltpu.VMEM((own, 2 * length), jnp.float32),
            pltpu.VMEM((branches * own, length), jnp.float32),
            pltpu.VMEM((2 * own, 2 * length), half),
            pltpu.VMEM((chips, 2, own, rows), half),
            pltpu.VMEM((groups, own, rows), half),
            dma((2,)),
            dma((chips, 2)),
            dma((groups,)),
            pltpu.VMEM((PARTS, branches * own, length // PARTS), jnp.float32),
            pltpu.VMEM((planes, rows, wide), half),
            pltpu.VMEM((groups, rows, wide), half),
            pltpu.VMEM((2, chips, branches * own, depth), half),
            pltpu.VMEM((chips, branches * own, depth), half),
            pltpu.VMEM((PARTS, chips - 1, branches * own, length // PARTS), half),
            pltpu.VMEM((PARTS, chips - 1, branches * own, length // PARTS), half),
            dma((PARTS, planes)),
            dma((PARTS, planes)),
            dma((PARTS, planes)),
            dma((PARTS, chips)),
            dma((PARTS, chips)),
            dma((PARTS, chips)),
            dma,
            dma,
            dma((PARTS, chips - 1)),
            dma((PARTS, chips - 1)),
            dma((PARTS,)),
        ],
        compiler_params=pltpu.CompilerParams(
            collective_id=0, has_side_effects=True, vmem_limit_bytes=48 * 1024 * 1024
        ),
    )(tokens, w_proj.reshape(depth, branches * width), scalars, long_filter, *tables)


def by_tokens(tokens, w_proj, short_filter, long_filter, skip_gain):
    branches, width = w_proj.shape[1:]
    groups = lax.axis_size("seq")
    own = width // groups
    tables = tuple(jnp.asarray(part) for part in dft_tables(tokens.shape[0] * groups))
    first = lax.axis_index("seq") * own
    scalars = jnp.concatenate(
        [short_filter, jnp.broadcast_to(skip_gain, (branches, 1, width))], axis=1
    )
    scalars = lax.dynamic_slice_in_dim(scalars, first, own, axis=2)
    scalars = scalars.transpose(0, 2, 1).reshape(branches * own, -1)
    return operator_kernel(tokens, w_proj, scalars, long_filter, tables)


def on_device(tokens, w_proj, short_filter, long_filter, skip_gain):
    chips = lax.axis_size("mp")
    paired = lax.axis_size("seq") == 2 * chips and tokens.shape[1] == 2 * w_proj.shape[0]
    if paired and tokens.shape[0] < w_proj.shape[0]:
        return by_tokens(tokens, w_proj, short_filter, long_filter, skip_gain)
    return by_weights(tokens, w_proj, short_filter, long_filter, skip_gain)


def solution(mesh):
    return jax.shard_map(
        on_device,
        mesh=mesh,
        in_specs=(
            P("seq", "mp"),
            P("seq", None, "mp"),
            P(None, None, "mp"),
            P(("mp", "seq"), None),
            P("mp"),
        ),
        out_specs=P("seq", "mp"),
        check_vma=False,
    )
```

```python
import functools
import math

import jax
import jax.numpy as jnp
import numpy as np
from jax import lax
from jax.experimental import pallas as pl
from jax.experimental.pallas import tpu as pltpu
from jax.sharding import PartitionSpec as P


def shifted(value, axis, steps):
    count = lax.axis_size(axis)
    leading, last = (max(0, -steps), min(count, count - steps))
    return lax.ppermute(value, axis, [(source, source + steps) for source in range(leading, last)])


def transform(real_part, imag_part, orient, filled):
    length = real_part.shape[-1]
    first = math.gcd(length, 64)
    highest = lax.Precision.HIGHEST
    if length <= 64 or first == 1:
        counter = jnp.arange(length, dtype=jnp.int32)
        angles = (
            2.0
            * math.pi
            / length
            * (counter[:, None] * counter[None, :] % length).astype(jnp.float32)
        )
        cosine = jnp.cos(angles)
        sine = jnp.sin(angles)
        new_real = jnp.dot(real_part, cosine, precision=highest) - orient * jnp.dot(
            imag_part, sine, precision=highest
        )
        new_imag = jnp.dot(imag_part, cosine, precision=highest) + orient * jnp.dot(
            real_part, sine, precision=highest
        )
        return (new_real, new_imag)
    second = length // first
    outer = real_part.shape[:-1]
    live = first
    if filled > 0 and filled % second == 0:
        live = filled // second
    real_grid = real_part.reshape(outer + (first, second))[..., :live, :]
    imag_grid = imag_part.reshape(outer + (first, second))[..., :live, :]
    counter = jnp.arange(first, dtype=jnp.int32)
    angles = (
        2.0 * math.pi / first * (counter[:, None] * counter[None, :] % first).astype(jnp.float32)
    )
    cosine = jnp.cos(angles)[:live]
    sine = jnp.sin(angles)[:live]
    section_real = jnp.einsum(
        "...ab,ak->...kb", real_grid, cosine, precision=highest
    ) - orient * jnp.einsum("...ab,ak->...kb", imag_grid, sine, precision=highest)
    section_imag = jnp.einsum(
        "...ab,ak->...kb", imag_grid, cosine, precision=highest
    ) + orient * jnp.einsum("...ab,ak->...kb", real_grid, sine, precision=highest)
    freq_rows = jnp.arange(first, dtype=jnp.int32)[:, None]
    time_cols = jnp.arange(second, dtype=jnp.int32)[None, :]
    twiddle = 2.0 * math.pi / length * (freq_rows * time_cols).astype(jnp.float32)
    twist_cos = jnp.cos(twiddle)
    twist_sin = jnp.sin(twiddle)
    turned_real = section_real * twist_cos - orient * section_imag * twist_sin
    turned_imag = section_imag * twist_cos + orient * section_real * twist_sin
    inner_real, inner_imag = transform(turned_real, turned_imag, orient, 0)
    final_real = jnp.swapaxes(inner_real, -1, -2).reshape(outer + (length,))
    final_imag = jnp.swapaxes(inner_imag, -1, -2).reshape(outer + (length,))
    return (final_real, final_imag)


def mirrored(values):
    return jnp.concatenate([values[:, :1], values[:, :0:-1]], axis=1)


def long_conv(signal, kernel):
    seq_len = signal.shape[-1]
    padded_signal = jnp.pad(signal.astype(jnp.float32), ((0, 0), (0, seq_len)))
    padded_kernel = jnp.pad(kernel, ((0, 0), (0, seq_len)))
    joint_real, joint_imag = transform(padded_signal, padded_kernel, -1.0, seq_len)
    mirror_real = mirrored(joint_real)
    mirror_imag = mirrored(joint_imag)
    signal_real = 0.5 * (joint_real + mirror_real)
    signal_imag = 0.5 * (joint_imag - mirror_imag)
    kernel_real = 0.5 * (joint_imag + mirror_imag)
    kernel_imag = -0.5 * (joint_real - mirror_real)
    prod_real = signal_real * kernel_real - signal_imag * kernel_imag
    prod_imag = signal_real * kernel_imag + signal_imag * kernel_real
    back_real, back_imag = transform(prod_real, prod_imag, 1.0, 0)
    return back_real[:, :seq_len] / (2.0 * seq_len)


def by_weights(tokens, w_proj, short_filter, long_filter, skip_gain):
    rows_dev = tokens.shape[0]
    margin = short_filter.shape[1] - 1
    width = w_proj.shape[2]
    source = lax.all_gather(tokens, "mp", axis=1, tiled=True)
    projected = jnp.einsum(
        "td,dpc->tpc",
        source,
        lax.all_gather(w_proj, "seq", axis=0, tiled=True),
        preferred_element_type=jnp.float32,
    ).astype(jnp.bfloat16)
    tail = shifted(projected[rows_dev - margin :], "seq", 1)
    extended = jnp.concatenate([tail, projected], axis=0).astype(jnp.float32)
    mixed = jnp.zeros((rows_dev, 3, width), jnp.float32)
    for offset in range(margin + 1):
        mixed = (
            mixed
            + short_filter[:, offset, :][None]
            * extended[margin - offset : margin - offset + rows_dev]
        )
    query_rows = mixed[:, 0]
    product = (mixed[:, 1] * mixed[:, 2]).astype(jnp.bfloat16)
    groups = lax.axis_size("seq")
    channel_count = width // groups
    outgoing = product.reshape(rows_dev, groups, channel_count).transpose(1, 2, 0)
    arrived = lax.all_to_all(outgoing, "seq", split_axis=0, concat_axis=2, tiled=True)[0]
    convolved = long_conv(arrived, long_filter).astype(jnp.bfloat16)[None]
    returned = lax.all_to_all(convolved, "seq", split_axis=2, concat_axis=0, tiled=True)
    back_rows = returned.transpose(2, 0, 1).reshape(rows_dev, width)
    result = query_rows * (
        back_rows.astype(jnp.float32) + skip_gain[None, :] * product.astype(jnp.float32)
    )
    return result.astype(jnp.bfloat16)


def split_float(value):
    high = value.astype(jnp.bfloat16)
    low = (value - high.astype(jnp.float32)).astype(jnp.bfloat16)
    return high, low


def dft_tables(length):
    phase = (4 * np.arange(length)[:, None] + 1) * np.arange(length)[None, :] % (4 * length)
    angles = phase * (2.0 * np.pi / (4 * length))
    table = np.concatenate([np.cos(angles), np.sin(angles)], axis=0).astype(np.float32)
    high = table.astype(jnp.bfloat16)
    low = (table - high.astype(np.float32)).astype(jnp.bfloat16)
    return high, low


def matmul_t(left, right):
    return lax.dot_general(
        left, right, (((1,), (1,)), ((), ())), preferred_element_type=jnp.float32
    )


def matmul(left, right):
    return jnp.dot(left, right, preferred_element_type=jnp.float32)


MESH = pl.DeviceIdType.MESH
PARTS = 2


def project_kernel(
    planes,
    chips,
    branches,
    tokens,
    weights_far,
    scalars,
    kernel,
    high_table,
    low_table,
    out,
    weights,
    high,
    low,
    spectrum,
    projected,
    spectral,
    leaving,
    collected,
    t_sem,
    a_send,
    a_recv,
    total,
    gathered,
    features,
    packed,
    paired,
    partial,
    arrived,
    z_send,
    z_recv,
    f_send,
    f_recv,
    p_send,
    p_recv,
    w_send,
    w_recv,
    r_send,
    r_recv,
    own_sem,
):
    place = lax.axis_index("seq")
    plane = lax.axis_index("mp")
    chip, core = place // 2, lax.rem(place, 2)
    rows, depth = tokens.shape[0], weights.shape[1]
    width = weights.shape[2]
    own = width // (2 * chips)
    sibling = (chip * 2 + 1 - core, plane)

    barrier = pltpu.get_barrier_semaphore()
    partners = [(place, lax.rem(plane + step, planes)) for step in range(1, planes)]
    partners += [(lax.rem(chip + step, chips) * 2 + core, plane) for step in range(1, chips)]
    partners += [(lax.rem(chip + step, chips) * 2 + 1 - core, plane) for step in range(chips)]
    for partner in partners:
        pl.semaphore_signal(barrier, inc=1, device_id=partner, device_id_type=MESH)
    pl.semaphore_wait(barrier, len(partners))

    def remote(source, target, send, recv, device):
        return pltpu.make_async_remote_copy(
            src_ref=source,
            dst_ref=target,
            send_sem=send,
            recv_sem=recv,
            device_id=device,
            device_id_type=MESH,
        )

    share = rows // PARTS
    weight_copy = pltpu.make_async_copy(weights_far, weights, t_sem.at[2])
    table_copies = [
        pltpu.make_async_copy(high_table, high, t_sem.at[0]),
        pltpu.make_async_copy(low_table, low, t_sem.at[1]),
    ]

    def cut(ref, part):
        return ref.at[part * share : (part + 1) * share]

    def along_z(part):
        copies = []
        for step in range(1, planes):
            copy = remote(
                cut(tokens, part),
                cut(gathered.at[plane], part),
                z_send.at[part, step],
                z_recv.at[part, plane],
                (place, lax.rem(plane + step, planes)),
            )
            copy.start()
            copies.append(copy)
        return copies

    z_copies = along_z(0)
    for copy in [weight_copy] + table_copies:
        copy.start()
    gathered[plane] = tokens[...]

    def scatter_copy(part, step):
        slot = lax.rem(plane - step + planes, planes)
        return slot, remote(
            cut(gathered.at[slot], part),
            cut(features.at[place], part),
            f_send.at[part, step],
            f_recv.at[part, chip],
            (slot * 2 + core, plane),
        )

    def own_copy(part):
        return pltpu.make_async_copy(
            cut(gathered.at[chip], part), cut(features.at[place], part), own_sem.at[part]
        )

    def scatter(part, step):
        slot, copy = scatter_copy(part, step)
        if step:
            remote(
                cut(tokens, part),
                cut(gathered.at[slot], part),
                z_send.at[part, step],
                z_recv.at[part, slot],
                (place, slot),
            ).wait_recv()

        @pl.when(slot == chip)
        def _():
            own_copy(part).start()

        @pl.when(slot != chip)
        def _():
            copy.start()

    for part in range(PARTS):
        scatter(part, 0)

    weight_copy.wait()
    for branch in range(branches):
        turned = weights[branch].T
        for group in range(2 * chips):
            packed[group % 2, group // 2, branch * own : (branch + 1) * own, :] = turned[
                group * own : (group + 1) * own
            ]
    w_copy = remote(packed.at[1 - core], paired, w_send, w_recv, sibling)
    w_copy.start()
    for part in range(1, PARTS):
        for copy in z_copies[-(planes - 1) :]:
            copy.wait_send()
        z_copies += along_z(part)

    for copy in table_copies:
        copy.wait()
    length = kernel.shape[1]
    chunk = 2 * rows
    kernel_high, kernel_low = split_float(kernel[...])
    kernel_both = jnp.concatenate([kernel_high, kernel_low], axis=0)

    def transform_filter(block, carry):
        at = pl.ds(pl.multiple_of(block * chunk, chunk), chunk)
        both = matmul_t(kernel_both, high[at, :])
        spectrum[:, at] = both[:own] + both[own:] + matmul_t(kernel_high, low[at, :])
        return carry

    lax.fori_loop(0, 2 * length // chunk, transform_filter, 0)

    p_copies, r_copies = [], []
    here = pl.ds(pl.multiple_of(core * depth, depth), depth)
    there = pl.ds(pl.multiple_of((1 - core) * depth, depth), depth)

    def forward(part):
        for step in range(chips):
            source = lax.rem(chip + step, chips)
            piece = cut(features.at[source * 2 + core], part)
            if step == 0:
                own_copy(part).wait()
            else:
                remote(
                    cut(gathered.at[0], part),
                    piece,
                    f_send.at[part, 0],
                    f_recv.at[part, source],
                    (source * 2 + core, plane),
                ).wait_recv()
            copy = remote(piece, piece, p_send.at[part, step], p_recv.at[part, source], sibling)
            copy.start()
            p_copies.append(copy)

    span = 2 * chips // 2
    across = span * share

    def push(part):
        if part == 0:
            w_copy.wait_recv()
        for step in range(chips):
            source = lax.rem(chip + step, chips)
            piece = cut(features.at[source * 2 + 1 - core], part)
            remote(piece, piece, p_send.at[part, step], p_recv.at[part, source], sibling).wait_recv()

        def product(target, block):
            which = (pl.ds(block * span, span), slice(part * share, (part + 1) * share))
            near = features[(*which, here)].reshape(across, depth)
            far = features[(*which, there)].reshape(across, depth)
            return matmul_t(packed[core, target], near) + matmul_t(paired[target], far)

        for step in list(range(1, chips)) + [0]:
            target = lax.rem(chip + step, chips)

            def fill(block, carry, target=target, step=step):
                columns = pl.ds(pl.multiple_of(block * across, across), across)
                value = product(target, block)
                if step:
                    partial[part, step - 1, :, columns] = value.astype(jnp.bfloat16)
                else:
                    total[part, :, columns] = value
                return carry

            lax.fori_loop(0, 2, fill, 0)
            if step:
                copy = remote(
                    partial.at[part, step - 1],
                    arrived.at[part, step - 1],
                    r_send.at[part, step - 1],
                    r_recv.at[part, step - 1],
                    (target * 2 + core, plane),
                )
                copy.start()
                r_copies.append(copy)

    for step in range(1, planes):
        scatter(0, step)
    forward(0)
    for part in range(PARTS):
        if part + 1 < PARTS:
            for step in range(1, planes):
                scatter(part + 1, step)
        push(part)
        if part + 1 < PARTS:
            forward(part + 1)

    for copy in r_copies:
        copy.wait_recv()

    left = lax.broadcasted_iota(jnp.int32, (branches * own, rows), 1) < share

    def add(pair, carry):
        columns = pl.ds(pl.multiple_of(pair * rows, rows), rows)
        values = []
        for part in range(PARTS):
            value = total[part, :, columns]
            for step in range(chips - 1):
                value = value + arrived[part, step, :, columns].astype(jnp.float32)
            values.append(value)
        first = jnp.where(left, values[0], pltpu.roll(values[1], share, 1))
        second = jnp.where(left, pltpu.roll(values[0], share, 1), values[1])
        at = pl.multiple_of(pair * 2 * rows, 2 * rows)
        near, far = pl.ds(at, rows), pl.ds(pl.multiple_of(at + rows, rows), rows)
        projected[:, near] = first.astype(jnp.bfloat16).astype(jnp.float32)
        projected[:, far] = second.astype(jnp.bfloat16).astype(jnp.float32)
        return carry

    lax.fori_loop(0, chips, add, 0)

    token = lax.broadcasted_iota(jnp.int32, (own, length), 1)
    mixed = []
    for branch in range(branches):
        at = slice(branch * own, (branch + 1) * own)
        value = projected[at, :]
        result = scalars[at, 0:1] * value
        for offset in range(1, scalars.shape[1] - 1):
            moved = jnp.where(token >= offset, pltpu.roll(value, offset, 1), 0.0)
            result = result + scalars[at, offset : offset + 1] * moved
        mixed.append(result)
    signal = (mixed[1] * mixed[2]).astype(jnp.bfloat16)
    gain = scalars[0:own, scalars.shape[1] - 1 :]
    projected[0:own, :] = mixed[0]
    projected[own : 2 * own, :] = gain * signal.astype(jnp.float32)

    for block in range(length // chunk):
        real_at = slice(block * chunk, (block + 1) * chunk)
        imag_at = slice(length + block * chunk, length + (block + 1) * chunk)
        own_real = matmul_t(signal, high[real_at, :]) + matmul_t(signal, low[real_at, :])
        own_imag = matmul_t(signal, high[imag_at, :]) + matmul_t(signal, low[imag_at, :])
        real, imag = spectrum[:, real_at], spectrum[:, imag_at]
        for at, value in (
            (real_at, own_real * real - own_imag * imag),
            (imag_at, own_real * imag + own_imag * real),
        ):
            value_high, value_low = split_float(value)
            spectral[0:own, at] = value_high
            spectral[own : 2 * own, at] = value_low

    a_copies = []
    for step in list(range(1, chips)) + [0]:
        target = lax.rem(chip + step, chips)
        at = pl.ds(pl.multiple_of(target * chunk, chunk), chunk)
        both = matmul(spectral[...], high[:, at])
        value = both[:own] + both[own:] + matmul(spectral[0:own, :], low[:, at])
        value = (value * (1.0 / length)).astype(jnp.bfloat16).astype(jnp.float32)
        value = (projected[0:own, at] * (value + projected[own : 2 * own, at])).astype(jnp.bfloat16)
        leaving[step, 0] = value[:, :rows]
        leaving[step, 1] = value[:, rows:]
        for other in (1, 0):
            side = core if other == 0 else 1 - core
            if step == 0 and other == 0:
                collected[place] = leaving[step, side]
                continue
            copy = remote(
                leaving.at[step, side],
                collected.at[place],
                a_send.at[step, other],
                a_recv.at[place],
                (target * 2 + side, plane),
            )
            copy.start()
            a_copies.append(copy)
    for step in range(1, 2 * chips):
        source = lax.rem(place + step, 2 * chips)
        remote(
            leaving.at[0, 0], collected.at[source], a_send.at[0, 0], a_recv.at[source], (source, plane)
        ).wait_recv()
    out[...] = collected[...].reshape(2 * chips * own, rows).T

    for copy in z_copies[-(planes - 1) :] + p_copies + [w_copy] + r_copies + a_copies:
        copy.wait_send()
    for part in range(PARTS):
        for step in range(planes):
            slot, copy = scatter_copy(part, step)

            @pl.when(slot != chip)
            def _(copy=copy):
                copy.wait_send()


def operator_kernel(tokens, w_proj, scalars, long_filter, tables):
    depth, branches, width = w_proj.shape
    rows, wide = tokens.shape
    groups, planes = lax.axis_size("seq"), lax.axis_size("mp")
    chips = groups // 2
    own = width // groups
    length = rows * groups
    dma = pltpu.SemaphoreType.DMA

    vmem = pl.BlockSpec(memory_space=pltpu.VMEM)
    far = pl.BlockSpec(memory_space=pl.ANY)
    half = jnp.bfloat16
    return pl.pallas_call(
        functools.partial(project_kernel, planes, chips, branches),
        out_shape=jax.ShapeDtypeStruct((rows, width), half),
        in_specs=[vmem, far, vmem, vmem, far, far],
        out_specs=vmem,
        scratch_shapes=[
            pltpu.VMEM((branches, depth, width), half),
            pltpu.VMEM((2 * length, length), half),
            pltpu.VMEM((2 * length, length), half),
            pltpu.VMEM((own, 2 * length), jnp.float32),
            pltpu.VMEM((branches * own, length), jnp.float32),
            pltpu.VMEM((2 * own, 2 * length), half),
            pltpu.VMEM((chips, 2, own, rows), half),
            pltpu.VMEM((groups, own, rows), half),
            dma((3,)),
            dma((chips, 2)),
            dma((groups,)),
            pltpu.VMEM((PARTS, branches * own, length // PARTS), jnp.float32),
            pltpu.VMEM((planes, rows, wide), half),
            pltpu.VMEM((groups, rows, wide), half),
            pltpu.VMEM((2, chips, branches * own, depth), half),
            pltpu.VMEM((chips, branches * own, depth), half),
            pltpu.VMEM((PARTS, chips - 1, branches * own, length // PARTS), half),
            pltpu.VMEM((PARTS, chips - 1, branches * own, length // PARTS), half),
            dma((PARTS, planes)),
            dma((PARTS, planes)),
            dma((PARTS, planes)),
            dma((PARTS, chips)),
            dma((PARTS, chips)),
            dma((PARTS, chips)),
            dma,
            dma,
            dma((PARTS, chips - 1)),
            dma((PARTS, chips - 1)),
            dma((PARTS,)),
        ],
        compiler_params=pltpu.CompilerParams(
            collective_id=0, has_side_effects=True, vmem_limit_bytes=48 * 1024 * 1024
        ),
    )(tokens, w_proj.transpose(1, 0, 2), scalars, long_filter, *tables)


def by_tokens(tokens, w_proj, short_filter, long_filter, skip_gain):
    branches, width = w_proj.shape[1:]
    groups = lax.axis_size("seq")
    own = width // groups
    tables = tuple(jnp.asarray(part) for part in dft_tables(tokens.shape[0] * groups))
    first = lax.axis_index("seq") * own
    scalars = jnp.concatenate(
        [short_filter, jnp.broadcast_to(skip_gain, (branches, 1, width))], axis=1
    )
    scalars = lax.dynamic_slice_in_dim(scalars, first, own, axis=2)
    scalars = scalars.transpose(0, 2, 1).reshape(branches * own, -1)
    return operator_kernel(tokens, w_proj, scalars, long_filter, tables)


def on_device(tokens, w_proj, short_filter, long_filter, skip_gain):
    chips = lax.axis_size("mp")
    paired = lax.axis_size("seq") == 2 * chips and tokens.shape[1] == 2 * w_proj.shape[0]
    if paired and tokens.shape[0] < w_proj.shape[0]:
        return by_tokens(tokens, w_proj, short_filter, long_filter, skip_gain)
    return by_weights(tokens, w_proj, short_filter, long_filter, skip_gain)


def solution(mesh):
    return jax.shard_map(
        on_device,
        mesh=mesh,
        in_specs=(
            P("seq", "mp"),
            P("seq", None, "mp"),
            P(None, None, "mp"),
            P(("mp", "seq"), None),
            P("mp"),
        ),
        out_specs=P("seq", "mp"),
        check_vma=False,
    )
```
